512 devices in a mesh: orb: 16 (over z_lo, core), aux: 32 (over x, y, z_hi).
Axes of the slice: x: 4, y: 4, z: 16 (z_hi: 2, z_lo: 8; z = z_hi * 8 + z_lo), core: 2. Of those that a mesh axis runs over, the one named last changes fastest.
Arguments:
- slab: float32 [512, 256, 256], P('aux', 'orb'), may hold values from -0.375 to 0.375
- pair_blocks: int32 [4, 4], replicated, may hold values from 0 to 1, as said below
- occ_density: float32 [2, 256, 256], P(None, 'orb'), may hold values from -0.375 to 0.375
- vir_density: float32 [2, 256, 256], replicated, may hold values from -0.375 to 0.375
Outputs:
- response: float32 [2, 512, 512], P(None, 'aux')
The draws below stay inside these ranges and needn't reach their ends.
Inputs may be any that keep to these rules, and one draw needn't show every extreme that they name: `pair_blocks`: blocks on the diagonal are always kept.
All inputs are finite; a program needn't handle non-finite values.
Results may differ from the reference program's by a relative error of at most 0.0001.
Values sent between devices are 32-bit elements; how exact they have to be, the bound alone decides.
No kernel may reach another device: no remote copies, remote signals or barrier semaphores. Data moves between devices by JAX's collectives and lax.ppermute only.
A program may use at most 64 MiB of HBM per device.

```python
import jax
import jax.numpy as jnp
from jax import lax

NAUX = 512
BLK = 64
NT = 2
NORB = 256


def draw_pair_blocks(key, part):
    key = jax.random.fold_in(key, 7)
    count = NORB // BLK
    random_bits = jax.random.randint(key, (count, count), 0, 2)
    return jnp.maximum(random_bits, jnp.eye(count, dtype=jnp.int32)).astype(jnp.int32)


def block_scale(stream_key, dims, pieces, least, high):
    factor_of, own = 1.0, jax.random.fold_in(stream_key, 6)
    for dim, shards_of in pieces:
        draws = jnp.exp(jax.random.uniform(jax.random.fold_in(own, dim), (shards_of,), jnp.float32, least / len(pieces), high / len(pieces)))
        factor_of = factor_of * jnp.repeat(draws, dims[dim] // shards_of).reshape([-1 if axis == dim else 1 for axis in range(len(dims))])
    return factor_of


def gaussian(key, shape, width, most, shards=(), held_as=jnp.bfloat16):
    gain = block_scale(key, shape, shards, -0.22, 0.18) if shards else 1.0
    result = jax.random.normal(key, shape, jnp.float32) * width * gain
    return jnp.minimum(jnp.maximum(result, -most), most).astype(held_as)


def setup_inputs(seed: int = 0) -> dict:
    seeds = jax.random.split(jax.random.key(seed), 5)
    return {
        "slab": gaussian(seeds[0], (NAUX, NORB, NORB), NORB ** -0.5, 0.375, ((0, 32), (1, 16)), jnp.float32),
        "pair_blocks": draw_pair_blocks(jax.random.fold_in(seeds[4], 71), 0),
        "occ_density": gaussian(seeds[2], (NT, NORB, NORB), NORB ** -0.5, 0.375, ((1, 16),), jnp.float32),
        "vir_density": gaussian(seeds[3], (NT, NORB, NORB), NORB ** -0.5, 0.375, (), jnp.float32),
    }


def reference(slab, pair_blocks, occ_density, vir_density):
    count = NORB // BLK
    expanded = jnp.broadcast_to(pair_blocks.astype(jnp.float32)[:, None, :, None], (count, BLK, count, BLK)).reshape(NORB, NORB)
    masked = slab * expanded[None]
    results = []
    for moment in range(NT):
        mixed_part = jnp.einsum('pmn,nb->pmb', masked, vir_density[moment], precision=lax.Precision.HIGHEST)
        paired = jnp.einsum('am,pmb->pab', occ_density[moment], mixed_part, precision=lax.Precision.HIGHEST)
        results.append(jnp.einsum('pab,qab->pq', paired, masked, precision=lax.Precision.HIGHEST))
    return jnp.stack(results)
```

```python
import jax
import jax.numpy as jnp
from jax import lax
from jax.experimental import pallas as pl
from jax.experimental.pallas import tpu as pltpu
from jax.sharding import Mesh, PartitionSpec as P

NT_DIMS = (((1,), (1,)), ((), ()))
NN_DIMS = (((1,), (0,)), ((), ()))


def split(value):
    high = value.astype(jnp.bfloat16)
    return high, (value - high.astype(jnp.float32)).astype(jnp.bfloat16)


def dot3(left, right, dims):
    left_high, left_low = split(left)
    right_high, right_low = split(right)

    def dot(a, b):
        return lax.dot_general(a, b, dims, preferred_element_type=jnp.float32)

    return dot(left_high, right_high) + (dot(left_low, right_high) + dot(left_high, right_low))


def pairing(times, slab_ref, vir_ref, occ_ref, out_ref):
    peers, _, rows, width = out_ref.shape
    slab = slab_ref[...].reshape(vir_ref.shape[1:])
    for t in range(times):
        mixed = dot3(slab, vir_ref[t], NN_DIMS)
        paired = dot3(occ_ref[t], mixed, NN_DIMS)
        out_ref[:, t] = paired.reshape(peers, rows, width)


def respond(paired_ref, slab_ref, out_ref):
    step = pl.program_id(0)
    sources, times = paired_ref.shape[:2]
    halves, _, count, width = slab_ref.shape
    run = count // 16
    right = slab_ref[...].reshape(halves, 16, run, width)
    right = jnp.swapaxes(right, 0, 1).reshape(halves * count, width)
    left = jnp.concatenate([paired_ref[:, t, pl.ds(step, 1), :].reshape(sources, width) for t in range(times)], axis=0)
    total = dot3(left, right, NT_DIMS)
    lanes = out_ref.shape[2]

    @pl.when(step == 0)
    def _():
        out_ref[...] = jnp.zeros_like(out_ref)

    pieces = total.shape[1] // lanes
    for t in range(times):
        for k in range(pieces):
            out_ref[:, t * pieces + k, :] += total[t * sources:(t + 1) * sources, k * lanes:(k + 1) * lanes]


def body(slab, pair_blocks, occ_density, vir_density):
    aux_here, rows_here, norbit = slab.shape
    times = occ_density.shape[0]
    near, cores, planes, halves = 8, 2, 16, 2
    count = pair_blocks.shape[0]
    width = norbit // count
    block = lax.axis_index(("zl", "c")) * rows_here // width
    row_mask = jnp.repeat(lax.dynamic_index_in_dim(pair_blocks, block, 0, keepdims=False).astype(jnp.float32), width)
    masked = slab * row_mask[None, None, :]

    by_row = lax.all_to_all(jnp.swapaxes(masked, 0, 1), ("x", "y"), 0, 0, tiled=True)
    by_row = by_row.reshape(planes * aux_here, norbit)
    gathered = lax.all_gather(by_row, ("zh", "zl"), axis=0, tiled=True)
    gathered = gathered.reshape(halves, near, planes * aux_here, norbit)

    occ_all = lax.all_gather(occ_density, ("zl", "c"), axis=0, tiled=False)
    occ_all = occ_all.reshape(near, cores, times, rows_here, norbit).transpose(2, 1, 3, 0, 4).reshape(times, norbit, norbit)
    own = lax.all_to_all(masked, ("zl", "c"), 0, 0, tiled=True)
    vmem = pl.BlockSpec(memory_space=pltpu.VMEM)
    paired = pl.pallas_call(
        lambda *refs: pairing(times, *refs),
        out_shape=jax.ShapeDtypeStruct((cores * planes, times, near, norbit), jnp.float32),
        in_specs=[vmem, vmem, vmem],
        out_specs=vmem,
        compiler_params=pltpu.CompilerParams(vmem_limit_bytes=32 << 20),
        cost_estimate=pl.CostEstimate(flops=12 * times * norbit**3, bytes_accessed=2 << 20, transcendentals=0),
    )(own, vir_density, occ_all)
    paired = lax.all_to_all(paired.reshape(cores * planes, times * near, norbit), ("c", "x", "y"), 0, 0, tiled=True)
    paired = paired.reshape(cores * planes, times, near, norbit)

    total_aux = halves * planes * aux_here
    lanes = 128
    partial = pl.pallas_call(
        respond,
        grid=(near,),
        out_shape=jax.ShapeDtypeStruct((cores * planes, times * total_aux // lanes, lanes), jnp.float32),
        in_specs=[
            pl.BlockSpec((cores * planes, times, near, norbit), lambda s: (0, 0, 0, 0)),
            pl.BlockSpec((halves, 1, planes * aux_here, norbit), lambda s: (0, s, 0, 0)),
        ],
        out_specs=pl.BlockSpec((cores * planes, times * total_aux // lanes, lanes), lambda s: (0, 0, 0)),
        compiler_params=pltpu.CompilerParams(vmem_limit_bytes=32 << 20),
        cost_estimate=pl.CostEstimate(flops=1 << 28, bytes_accessed=5 << 20, transcendentals=0),
    )(paired, gathered)
    rows = jnp.sum(lax.all_to_all(partial, ("c", "x", "y"), 0, 0, tiled=True), axis=0)
    spread = jnp.broadcast_to(rows[None], (near * cores,) + rows.shape)
    everyone = lax.all_to_all(spread, ("zl", "c"), 0, 0, tiled=True)
    return jnp.swapaxes(everyone.reshape(aux_here, times, total_aux), 0, 1)


def solution(mesh):
    fine = Mesh(mesh.devices.reshape(8, 2, 4, 4, 2), ("zl", "c", "x", "y", "zh"))
    orb, aux = ("zl", "c"), ("x", "y", "zh")
    in_specs = (P(aux, orb, None), P(), P(None, orb, None), P())
    out_specs = P(None, aux, None)
    return jax.shard_map(body, mesh=fine, in_specs=in_specs, out_specs=out_specs, check_vma=False)
```

```python
import jax
import jax.numpy as jnp
from jax import lax
from jax.experimental import pallas as pl
from jax.experimental.pallas import tpu as pltpu
from jax.sharding import Mesh, PartitionSpec as P

NT_DIMS = (((1,), (1,)), ((), ()))
NN_DIMS = (((1,), (0,)), ((), ()))
LANES = 128
VMEM = pl.BlockSpec(memory_space=pltpu.VMEM)
SMEM = pl.BlockSpec(memory_space=pltpu.SMEM)
PARAMS = pltpu.CompilerParams(vmem_limit_bytes=32 << 20)
WIDE = pltpu.CompilerParams(vmem_limit_bytes=60 << 20)


def split(value):
    high = value.astype(jnp.bfloat16)
    return high, (value - high.astype(jnp.float32)).astype(jnp.bfloat16)


def dot3(left, right, dims):
    def dot(a, b):
        return lax.dot_general(a, b, dims, preferred_element_type=jnp.float32)

    return dot(left[0], right[0]) + (dot(left[1], right[0]) + dot(left[0], right[1]))


def block_row(blocks_ref, block, norbit):
    count = blocks_ref.shape[1]
    lane = lax.broadcasted_iota(jnp.int32, (1, norbit), 1) // (norbit // count)
    mask = jnp.zeros((1, norbit), jnp.float32)
    for k in range(count):
        mask = jnp.where(lane == k, blocks_ref[block, k].astype(jnp.float32), mask)
    return mask


def by_rows(blocks_ref, slab_ref, rows_ref):
    _, own_rows, norbit = slab_ref.shape
    place = (lax.axis_index("g") * 2 + lax.axis_index("b")) * 2 + lax.axis_index("c")
    mask = block_row(blocks_ref, lax.div(place * own_rows, norbit // blocks_ref.shape[0]), norbit)
    for m in range(own_rows):
        rows_ref[m] = slab_ref[:, m, :] * mask


def pairing(blocks_ref, slab_ref, occ_ref, vir_ref, out_ref):
    peers, times, rows, norbit = occ_ref.shape
    count = blocks_ref.shape[0]
    mask = jnp.concatenate(
        [jnp.broadcast_to(block_row(blocks_ref, j, norbit), (norbit // count, norbit)) for j in range(count)], axis=0
    )
    slab = split(slab_ref[...].reshape(norbit, norbit) * mask)
    dests = out_ref.shape[0]
    bands = norbit // dests
    for t in range(times):
        mixed = split(dot3(slab, split(vir_ref[t]), NN_DIMS))
        paired = dot3(split(occ_ref[:, t].reshape(norbit, norbit)), mixed, NN_DIMS)
        for g in range(bands):
            out_ref[:, t * bands + g, :] = paired[g * dests:(g + 1) * dests]


def respond(paired_ref, slab_ref, out_ref, total):
    step = pl.program_id(0)
    sources, planes = paired_ref.shape[0], 16
    halves, _, count, norbit = slab_ref.shape
    bands = pl.num_programs(0)
    run = count // planes

    @pl.when(step == 0)
    def _():
        total[...] = jnp.zeros_like(total)

    rows = [paired_ref[:, pl.ds(i * bands + step, 1), :].reshape(sources, norbit) for i in range(2)]
    right = jnp.swapaxes(slab_ref[...].reshape(halves, planes, run, norbit), 0, 1).reshape(halves * count, norbit)
    total[...] += dot3(split(jnp.concatenate(rows, axis=0)), split(right), NT_DIMS)

    @pl.when(step == bands - 1)
    def _():
        whole = total[...].reshape(2, sources, halves * count)
        chunks = whole.shape[-1] // LANES
        for i in range(2):
            for k in range(chunks):
                out_ref[:, i * chunks + k, :] = whole[i, :, k * LANES:(k + 1) * LANES]


def body(slab, pair_blocks, occ_density, vir_density):
    aux_here, own_rows, norbit = slab.shape
    times = occ_density.shape[0]
    bands, pairs, cores, planes, halves = 4, 2, 2, 16, 2
    dests = pairs * cores * planes
    orb, share, f32 = ("g", "b", "c"), ("b", "c", "x", "y"), jnp.float32

    by_row = pl.pallas_call(
        by_rows,
        out_shape=jax.ShapeDtypeStruct((own_rows, aux_here, norbit), f32),
        in_specs=[SMEM, VMEM],
        out_specs=VMEM,
        compiler_params=WIDE,
    )(pair_blocks, slab)
    own = lax.all_to_all(by_row, ("x", "y"), 0, 0, tiled=True).reshape(planes * aux_here, norbit)
    gathered = lax.all_gather(own, ("zh", "g"), axis=0, tiled=True).reshape(halves, bands, planes * aux_here, norbit)

    later, later_occ, own = lax.optimization_barrier((slab, occ_density, own))
    first = lax.all_to_all(later, orb, 0, 0, tiled=True)
    occ_all = lax.all_gather(later_occ, orb, axis=0, tiled=False)
    paired = pl.pallas_call(
        pairing,
        out_shape=jax.ShapeDtypeStruct((dests, 2 * bands, norbit), f32),
        in_specs=[SMEM, VMEM, VMEM, VMEM],
        out_specs=VMEM,
        compiler_params=PARAMS,
    )(pair_blocks, first, occ_all, vir_density)
    paired = lax.all_to_all(paired, share, 0, 0, tiled=True)

    total_aux = halves * planes * aux_here
    per_row = times * total_aux // LANES
    partial = pl.pallas_call(
        respond,
        grid=(bands,),
        out_shape=jax.ShapeDtypeStruct((dests, per_row, LANES), f32),
        in_specs=[
            pl.BlockSpec((dests, 2 * bands, norbit), lambda s: (0, 0, 0)),
            pl.BlockSpec((halves, 1, planes * aux_here, norbit), lambda s: (0, s, 0, 0)),
        ],
        out_specs=pl.BlockSpec((dests, per_row, LANES), lambda s: (0, 0, 0)),
        scratch_shapes=[pltpu.VMEM((2 * dests, total_aux), f32)],
        compiler_params=PARAMS,
    )(paired.reshape(dests, 2 * bands, norbit), gathered)
    summed = lax.all_to_all(partial, share, 0, 0, tiled=True)
    row = jnp.sum(summed, axis=0)
    spread = jnp.broadcast_to(row[None], (aux_here,) + row.shape)
    everyone = lax.all_to_all(spread, orb, 0, 0, tiled=True)
    return jnp.swapaxes(everyone.reshape(aux_here, times, total_aux), 0, 1)


def solution(mesh):
    fine = Mesh(mesh.devices.reshape(4, 2, 2, 4, 4, 2), ("g", "b", "c", "x", "y", "zh"))
    orb, aux = ("g", "b", "c"), ("x", "y", "zh")
    in_specs = (P(aux, orb, None), P(), P(None, orb, None), P())
    out_specs = P(None, aux, None)
    return jax.shard_map(body, mesh=fine, in_specs=in_specs, out_specs=out_specs, check_vma=False)
```

```python
import jax
import jax.numpy as jnp
from jax import lax
from jax.experimental import pallas as pl
from jax.experimental.pallas import tpu as pltpu
from jax.sharding import Mesh, PartitionSpec as P

NT_DIMS = (((1,), (1,)), ((), ()))
NN_DIMS = (((1,), (0,)), ((), ()))
LANES = 128
VMEM = pl.BlockSpec(memory_space=pltpu.VMEM)
SMEM = pl.BlockSpec(memory_space=pltpu.SMEM)
PARAMS = pltpu.CompilerParams(vmem_limit_bytes=32 << 20)
WIDE = pltpu.CompilerParams(vmem_limit_bytes=60 << 20)


def split(value):
    high = value.astype(jnp.bfloat16)
    return high, (value - high.astype(jnp.float32)).astype(jnp.bfloat16)


def dot3(left, right, dims):
    def dot(a, b):
        return lax.dot_general(a, b, dims, preferred_element_type=jnp.float32)

    return dot(left[0], right[0]) + (dot(left[1], right[0]) + dot(left[0], right[1]))


def block_row(blocks_ref, block, norbit):
    count = blocks_ref.shape[1]
    lane = lax.broadcasted_iota(jnp.int32, (1, norbit), 1) // (norbit // count)
    mask = jnp.zeros((1, norbit), jnp.float32)
    for k in range(count):
        mask = jnp.where(lane == k, blocks_ref[block, k].astype(jnp.float32), mask)
    return mask


def by_rows(blocks_ref, slab_ref, rows_ref):
    _, own_rows, norbit = slab_ref.shape
    place = (lax.axis_index("g") * 2 + lax.axis_index("b")) * 2 + lax.axis_index("c")
    mask = block_row(blocks_ref, lax.div(place * own_rows, norbit // blocks_ref.shape[0]), norbit)
    for m in range(own_rows):
        rows_ref[m] = slab_ref[:, m, :] * mask


def pairing(blocks_ref, slab_ref, occ_ref, vir_ref, out_ref):
    peers, times, rows, norbit = occ_ref.shape
    count = blocks_ref.shape[0]
    mask = jnp.concatenate(
        [jnp.broadcast_to(block_row(blocks_ref, j, norbit), (norbit // count, norbit)) for j in range(count)], axis=0
    )
    slab = split(slab_ref[...].reshape(norbit, norbit) * mask)
    dests = out_ref.shape[0]
    bands = norbit // dests
    for t in range(times):
        mixed = split(dot3(slab, split(vir_ref[t]), NN_DIMS))
        paired = dot3(split(occ_ref[:, t].reshape(norbit, norbit)), mixed, NN_DIMS)
        for g in range(bands):
            out_ref[:, t * bands + g, :] = paired[g * dests:(g + 1) * dests]


def respond(paired_ref, slab_ref, out_ref, held, sems):
    sources = paired_ref.shape[0]
    bands, halves, count, norbit = held.shape
    planes = 16
    run = count // planes
    copies = [pltpu.make_async_copy(slab_ref.at[:, g], held.at[g], sems.at[g]) for g in range(bands)]
    for copy in copies:
        copy.start()
    lefts = []
    for g in range(bands):
        lefts.append(split(jnp.concatenate([paired_ref[:, i * bands + g, :] for i in range(2)], axis=0)))
    total = None
    for g in range(bands):
        copies[g].wait()
        right = jnp.swapaxes(held[g].reshape(halves, planes, run, norbit), 0, 1).reshape(halves * count, norbit)
        part = dot3(lefts[g], split(right), NT_DIMS)
        total = part if total is None else total + part
    chunks = halves * count // LANES
    for i in range(2):
        for k in range(chunks):
            out_ref[:, i * chunks + k, :] = total[i * sources:(i + 1) * sources, k * LANES:(k + 1) * LANES]


def body(slab, pair_blocks, occ_density, vir_density):
    aux_here, own_rows, norbit = slab.shape
    times = occ_density.shape[0]
    bands, pairs, cores, planes, halves = 4, 2, 2, 16, 2
    dests = pairs * cores * planes
    orb, share, f32 = ("g", "b", "c"), ("b", "c", "x", "y"), jnp.float32

    by_row = pl.pallas_call(
        by_rows,
        out_shape=jax.ShapeDtypeStruct((own_rows, aux_here, norbit), f32),
        in_specs=[SMEM, VMEM],
        out_specs=VMEM,
        compiler_params=WIDE,
    )(pair_blocks, slab)
    own = lax.all_to_all(by_row, ("x", "y"), 0, 0, tiled=True).reshape(planes * aux_here, norbit)
    gathered = lax.all_gather(own, ("zh", "g"), axis=0, tiled=True).reshape(halves, bands, planes * aux_here, norbit)

    later, later_occ, own = lax.optimization_barrier((slab, occ_density, own))
    first = lax.all_to_all(later, orb, 0, 0, tiled=True)
    occ_all = lax.all_gather(later_occ, orb, axis=0, tiled=False)
    paired = pl.pallas_call(
        pairing,
        out_shape=jax.ShapeDtypeStruct((dests, 2 * bands, norbit), f32),
        in_specs=[SMEM, VMEM, VMEM, VMEM],
        out_specs=VMEM,
        compiler_params=PARAMS,
    )(pair_blocks, first, occ_all, vir_density)
    paired = lax.all_to_all(paired, share, 0, 0, tiled=True)

    total_aux = halves * planes * aux_here
    per_row = times * total_aux // LANES
    partial = pl.pallas_call(
        respond,
        out_shape=jax.ShapeDtypeStruct((dests, per_row, LANES), f32),
        in_specs=[VMEM, pl.BlockSpec(memory_space=pltpu.HBM)],
        out_specs=VMEM,
        scratch_shapes=[
            pltpu.VMEM((bands, halves, planes * aux_here, norbit), f32),
            pltpu.SemaphoreType.DMA((bands,)),
        ],
        compiler_params=pltpu.CompilerParams(vmem_limit_bytes=53 << 20),
    )(paired, gathered)
    summed = lax.all_to_all(partial, share, 0, 0, tiled=True)
    row = jnp.sum(summed, axis=0)
    spread = jnp.broadcast_to(row[None], (aux_here,) + row.shape)
    everyone = lax.all_to_all(spread, orb, 0, 0, tiled=True)
    return jnp.swapaxes(everyone.reshape(aux_here, times, total_aux), 0, 1)


def solution(mesh):
    fine = Mesh(mesh.devices.reshape(4, 2, 2, 4, 4, 2), ("g", "b", "c", "x", "y", "zh"))
    orb, aux = ("g", "b", "c"), ("x", "y", "zh")
    in_specs = (P(aux, orb, None), P(), P(None, orb, None), P())
    out_specs = P(None, aux, None)
    return jax.shard_map(body, mesh=fine, in_specs=in_specs, out_specs=out_specs, check_vma=False)
```

```python
import jax
import jax.numpy as jnp
from jax import lax
from jax.experimental import pallas as pl
from jax.experimental.pallas import tpu as pltpu
from jax.sharding import Mesh, PartitionSpec as P

NT_DIMS = (((1,), (1,)), ((), ()))
NN_DIMS = (((1,), (0,)), ((), ()))
LANES = 128
VMEM = pl.BlockSpec(memory_space=pltpu.VMEM)
SMEM = pl.BlockSpec(memory_space=pltpu.SMEM)
PARAMS = pltpu.CompilerParams(vmem_limit_bytes=32 << 20)
WIDE = pltpu.CompilerParams(vmem_limit_bytes=60 << 20)


def split(value):
    high = value.astype(jnp.bfloat16)
    return high, (value - high.astype(jnp.float32)).astype(jnp.bfloat16)


def dot3(left, right, dims):
    def dot(a, b):
        return lax.dot_general(a, b, dims, preferred_element_type=jnp.float32)

    return dot(left[0], right[0]) + (dot(left[1], right[0]) + dot(left[0], right[1]))


def block_row(blocks_ref, block, norbit):
    count = blocks_ref.shape[1]
    lane = lax.broadcasted_iota(jnp.int32, (1, norbit), 1) // (norbit // count)
    mask = jnp.zeros((1, norbit), jnp.float32)
    for k in range(count):
        mask = jnp.where(lane == k, blocks_ref[block, k].astype(jnp.float32), mask)
    return mask


def by_rows(blocks_ref, slab_ref, rows_ref):
    _, own_rows, norbit = slab_ref.shape
    place = (lax.axis_index("g") * 2 + lax.axis_index("b")) * 2 + lax.axis_index("c")
    mask = block_row(blocks_ref, lax.div(place * own_rows, norbit // blocks_ref.shape[0]), norbit)
    for m in range(own_rows):
        rows_ref[m] = slab_ref[:, m, :] * mask


def pairing(blocks_ref, slab_ref, occ_ref, vir_ref, out_ref, full):
    groups, peers, rows, norbit = occ_ref.shape
    times = vir_ref.shape[0]
    each = rows // times
    inner, bands = out_ref.shape[0], peers // out_ref.shape[0]
    count = blocks_ref.shape[0]
    mask = jnp.concatenate(
        [jnp.broadcast_to(block_row(blocks_ref, j, norbit), (norbit // count, norbit)) for j in range(count)], axis=0
    )
    slab = split(slab_ref[...].reshape(norbit, norbit) * mask)
    for t in range(times):
        mixed = split(dot3(slab, split(vir_ref[t]), NN_DIMS))
        occ = [occ_ref[:, :, t * each + r, :].reshape(groups * peers, norbit) for r in range(each)]
        full[t] = dot3(split(jnp.concatenate(occ, axis=0)), mixed, NN_DIMS).reshape(full.shape[1:])
        for r in range(each):
            for g in range(bands):
                for n in range(inner):
                    out_ref[n, :, r, t * bands + g, :] = full[t, r, :, g * inner + n, :]


def respond(paired_ref, slab_ref, out_ref, held, sems):
    sources = paired_ref.shape[0]
    bands, halves, count, norbit = held.shape
    planes = 16
    run = count // planes
    copies = [pltpu.make_async_copy(slab_ref.at[:, g], held.at[g], sems.at[g]) for g in range(bands)]
    for copy in copies:
        copy.start()
    lefts = []
    for g in range(bands):
        lefts.append(split(jnp.concatenate([paired_ref[:, i * bands + g, :] for i in range(2)], axis=0)))
    total = None
    for g in range(bands):
        copies[g].wait()
        right = jnp.swapaxes(held[g].reshape(halves, planes, run, norbit), 0, 1).reshape(halves * count, norbit)
        part = dot3(lefts[g], split(right), NT_DIMS)
        total = part if total is None else total + part
    chunks = halves * count // LANES
    for i in range(2):
        for k in range(chunks):
            out_ref[:, i * chunks + k, :] = total[i * sources:(i + 1) * sources, k * LANES:(k + 1) * LANES]


def body(slab, pair_blocks, occ_density, vir_density):
    aux_here, own_rows, norbit = slab.shape
    times = occ_density.shape[0]
    bands, pairs, cores, planes, halves = 4, 2, 2, 16, 2
    dests = pairs * cores * planes
    orb, share, f32 = ("g", "b", "c"), ("b", "c", "xa", "xb", "y"), jnp.float32

    by_row = pl.pallas_call(
        by_rows,
        out_shape=jax.ShapeDtypeStruct((own_rows, aux_here, norbit), f32),
        in_specs=[SMEM, VMEM],
        out_specs=VMEM,
        compiler_params=WIDE,
    )(pair_blocks, slab)
    own = lax.all_to_all(by_row, ("xa", "xb", "y"), 0, 0, tiled=True).reshape(planes * aux_here, norbit)
    gathered = lax.all_gather(own, ("zh", "g"), axis=0, tiled=True).reshape(halves, bands, planes * aux_here, norbit)

    later, later_occ, own = lax.optimization_barrier((slab, occ_density, own))
    first = lax.all_to_all(later, orb, 0, 0, tiled=True)
    groups, peers = 2, bands * pairs * cores
    each = own_rows // groups
    mine = lax.dynamic_slice_in_dim(later_occ, lax.axis_index("xb") * each, each, 1).reshape(times * each, norbit)
    occ_all = lax.all_gather(lax.all_gather(mine, orb, axis=0, tiled=False), "xb", axis=0, tiled=False)
    paired = pl.pallas_call(
        pairing,
        out_shape=jax.ShapeDtypeStruct((pairs * cores, groups, each, times * bands, norbit), f32),
        in_specs=[SMEM, VMEM, VMEM, VMEM],
        out_specs=VMEM,
        scratch_shapes=[pltpu.VMEM((times, each, groups, peers, norbit), f32)],
        compiler_params=PARAMS,
    )(pair_blocks, first, occ_all, vir_density).reshape(dests, times * bands, norbit)
    paired = lax.all_to_all(paired, share, 0, 0, tiled=True)

    total_aux = halves * planes * aux_here
    per_row = times * total_aux // LANES
    partial = pl.pallas_call(
        respond,
        out_shape=jax.ShapeDtypeStruct((dests, per_row, LANES), f32),
        in_specs=[VMEM, pl.BlockSpec(memory_space=pltpu.HBM)],
        out_specs=VMEM,
        scratch_shapes=[
            pltpu.VMEM((bands, halves, planes * aux_here, norbit), f32),
            pltpu.SemaphoreType.DMA((bands,)),
        ],
        compiler_params=pltpu.CompilerParams(vmem_limit_bytes=53 << 20),
    )(paired, gathered)
    summed = lax.all_to_all(partial, share, 0, 0, tiled=True)
    row = jnp.sum(summed, axis=0)
    spread = jnp.broadcast_to(row[None], (aux_here,) + row.shape)
    everyone = lax.all_to_all(spread, orb, 0, 0, tiled=True)
    return jnp.swapaxes(everyone.reshape(aux_here, times, total_aux), 0, 1)


def solution(mesh):
    fine = Mesh(mesh.devices.reshape(4, 2, 2, 2, 2, 4, 2), ("g", "b", "c", "xa", "xb", "y", "zh"))
    orb, aux = ("g", "b", "c"), ("xa", "xb", "y", "zh")
    in_specs = (P(aux, orb, None), P(), P(None, orb, None), P())
    out_specs = P(None, aux, None)
    return jax.shard_map(body, mesh=fine, in_specs=in_specs, out_specs=out_specs, check_vma=False)
```
